32 devices in a mesh: row: 8 (over z, x), col: 4 (over y, core).
Axes of the slice: x: 2, y: 2, z: 4, core: 2. Of those that a mesh axis runs over, the one named last changes fastest.
Arguments:
- amplitudes: bfloat16 [1024, 16384], P(('row', 'col')), may hold values from -6 to 6
- integrals: bfloat16 [16384, 1024], P('row', 'col'), may hold values from -0.125 to 0.125
- vir_irrep: int32 [1024], replicated, may hold values from 0 to 7, as said below
- occ_starts: int32 [7], replicated, may hold values from 1 to 119, as said below
- panel_owner: int32 [8, 4], replicated, may hold values from 0 to 3, each once within a row
Outputs:
- residual: float32 [1024, 1024], P(('row', 'col'))
The draws below stay inside these ranges and needn't reach their ends.
Inputs may be any that keep to these rules, and one draw needn't show every extreme that they name: `vir_irrep`: each irrep labels exactly 128 virtual orbitals. `occ_starts`: strictly increasing; orbitals of irrep 0 start at 0. `panel_owner`: each row names each column index once.
All inputs are finite; a program needn't handle non-finite values.
Results may differ from the reference program's by a relative error of at most 0.0003.
Values may be sent and summed in bfloat16 or wider, within the bound.
A program may use at most 64 MiB of HBM per device.

```python
import math
import jax
import jax.numpy as jnp
from jax import lax

IRREPS = 8
NOCC = 120
NV = 1024
A_SLAB = 1
NQ = 1024
C_SLAB = 16
NK = 16384
NX = 1024
N_ROW = 8
N_COL = 4


def draw_vir_irrep(key, part):
    key = jax.random.fold_in(key, 5)
    shuffled = jax.random.permutation(key, NV)
    return (shuffled % IRREPS).astype(jnp.int32)


def draw_occ_starts(key, part):
    key = jax.random.fold_in(key, 11)
    shuffled = jax.random.permutation(key, NOCC - 3) + 2
    inner = shuffled[:IRREPS - 3]
    ends = jnp.array([1, NOCC - 1], dtype=jnp.int32)
    return jnp.sort(jnp.concatenate([inner.astype(jnp.int32), ends])).astype(jnp.int32)


def levels(stream_key, extent, split, least, largest):
    factor_of, own = 1.0, jax.random.fold_in(stream_key, 6)
    for axis_at, blocks in split:
        draws = jnp.exp(jax.random.uniform(jax.random.fold_in(own, axis_at), (blocks,), jnp.float32, least / len(split), largest / len(split)))
        factor_of = factor_of * jnp.repeat(draws, extent[axis_at] // blocks).reshape([-1 if axis == axis_at else 1 for axis in range(len(extent))])
    return factor_of


def scatter_about(own_key, dims, scale, bound, shards=(), kind=jnp.bfloat16):
    result = jax.random.normal(own_key, dims, jnp.float32) * scale
    if len(shards) > 0:
        result = levels(own_key, dims, shards, -0.22, 0.18) * result
    return jnp.clip(result, min=-bound, max=bound).astype(kind)


def setup_inputs(seed: int = 0) -> dict:
    key_of = jax.random.split(jax.random.key(seed), 6)
    amplitudes = scatter_about(key_of[0], (NQ, NK), 1.0, 6.0, ((0, 32),))
    integrals = scatter_about(key_of[1], (NK, NX), (NK // IRREPS) ** -0.5, 0.125, ((0, 8), (1, 4)))
    vir_irrep = draw_vir_irrep(jax.random.fold_in(key_of[5], 71), 0)
    occ_starts = draw_occ_starts(jax.random.fold_in(key_of[5], 71), 0)
    panel_owner = jax.vmap(lambda own: jax.random.permutation(own, N_COL))(jax.random.split(key_of[4], N_ROW)).reshape((N_ROW, N_COL)).astype(jnp.int32)
    return dict(amplitudes=amplitudes, integrals=integrals, vir_irrep=vir_irrep, occ_starts=occ_starts, panel_owner=panel_owner)


def occ_labels(orbital, occ_starts):
    return jnp.sum((orbital[:, None] >= occ_starts[None, :]).astype(jnp.int32), axis=1)


def pair_irreps(first_labels, vir_irrep):
    return jnp.bitwise_xor(first_labels[:, None], vir_irrep[None, :]).reshape(-1)


def reference(amplitudes, integrals, vir_irrep, occ_starts, panel_owner):
    panel_width = NX // N_COL
    blocks = integrals.reshape(N_ROW, NK // N_ROW, N_COL, panel_width)
    ordered = jnp.take_along_axis(blocks, panel_owner[:, None, :, None], axis=2).reshape(NK, NX)
    slab_irrep = pair_irreps(vir_irrep[:C_SLAB], vir_irrep)
    out_irrep = pair_irreps(vir_irrep[:A_SLAB], vir_irrep)
    masked_v = jnp.where(slab_irrep[:, None] == out_irrep[None, :], ordered, jnp.zeros((), ordered.dtype))
    block_rows = math.gcd(NQ, 1024)

    def one_block(first_row):
        pair_index = first_row + jnp.arange(block_rows, dtype=jnp.int32)
        pair_irrep = jnp.bitwise_xor(occ_labels(pair_index // NOCC, occ_starts), occ_labels(pair_index % NOCC, occ_starts))
        row_block = lax.dynamic_slice_in_dim(amplitudes, first_row, block_rows, 0)
        masked_t = jnp.where(pair_irrep[:, None] == slab_irrep[None, :], row_block, jnp.zeros((), row_block.dtype))
        return jnp.dot(masked_t, masked_v, preferred_element_type=jnp.float32)

    block_starts = jnp.arange(NQ // block_rows, dtype=jnp.int32) * block_rows
    return lax.map(one_block, block_starts).reshape(NQ, NX)
```

```python
import functools

import jax
import jax.numpy as jnp
from jax import lax
from jax.experimental import pallas as pl
from jax.experimental.pallas import tpu as pltpu
from jax.sharding import PartitionSpec as P

IRREPS = 8
NOCC = 120
MESH = pl.DeviceIdType.MESH
F32 = jnp.float32
BF16 = jnp.bfloat16


def dot(a, b):
    return jnp.dot(a, b, preferred_element_type=F32)


def dot_nt(a, b):
    return lax.dot_general(a, b, (((1,), (1,)), ((), ())), preferred_element_type=F32)


def three_parts(x):
    high = x.astype(BF16)
    rest = x - high.astype(F32)
    middle = rest.astype(BF16)
    low = (rest - middle.astype(F32)).astype(BF16)
    return high, middle, low


def kernel(
    rows, cols, live,
    amp_hbm, int_hbm, vir_ref, vir_s, occ_s, owner_s,
    out_ref,
    amp, integ, tsend, tbuf, vbuf, rpart, rrecv,
    load_sem, t_send, t_recv, v_send, v_recv, r_send, r_recv,
):
    row, col = lax.axis_index("row"), lax.axis_index("col")
    pair_rows, amp_cols = amp_hbm.shape
    slab_rows, panel = int_hbm.shape
    nvir = vir_ref.shape[1]
    local_c = slab_rows // nvir
    chips = cols // 2
    chip, core = col // 2, col % 2

    load_v = pltpu.make_async_copy(int_hbm, integ, load_sem.at[0])
    load_t = pltpu.make_async_copy(amp_hbm, amp, load_sem.at[1])
    load_v.start()
    load_t.start()

    barrier = pltpu.get_barrier_semaphore()
    for o in range(1, rows):
        pl.semaphore_signal(barrier, inc=1, device_id=(lax.rem(row + o, rows), col), device_id_type=MESH)
    for o in range(1, cols):
        pl.semaphore_signal(barrier, inc=1, device_id=(row, lax.rem(col + o, cols)), device_id_type=MESH)

    vir = vir_ref[...]
    irrep_of = lax.broadcasted_iota(jnp.int32, (IRREPS, nvir), 0)
    onehot = (jnp.broadcast_to(vir, (IRREPS, nvir)) == irrep_of).astype(F32)
    tiles = nvir // 128
    onehot_tiles = [onehot[:, i * 128:(i + 1) * 128] for i in range(tiles)]
    before = (
        lax.broadcasted_iota(jnp.int32, (128, 128), 0) < lax.broadcasted_iota(jnp.int32, (128, 128), 1)
    ).astype(BF16)
    within = dot(jnp.concatenate(onehot_tiles, axis=0).astype(BF16), before)
    carry = jnp.zeros((IRREPS, 1), F32)
    rank_tiles = []
    for i in range(tiles):
        counted = within[i * IRREPS:(i + 1) * IRREPS] + carry
        rank_tiles.append(jnp.sum(onehot_tiles[i] * counted, axis=0, keepdims=True))
        carry = carry + jnp.sum(onehot_tiles[i], axis=1, keepdims=True)
    rank = jnp.concatenate(rank_tiles, axis=1).astype(jnp.int32)

    def placed(row_of_ranks):
        width = row_of_ranks.shape[1]
        return (
            jnp.broadcast_to(row_of_ranks, (live, width)) == lax.broadcasted_iota(jnp.int32, (live, width), 0)
        ).astype(F32).astype(BF16)

    place = placed(rank)

    def panel_of(values, owner):
        result = jnp.zeros((1, panel), jnp.int32)
        for slot in range(cols):
            held = (owner_s[row, slot] == owner).astype(jnp.int32)
            result = result + held * values[:, slot * panel:(slot + 1) * panel]
        return result

    def pair_irrep(first, count):
        q = first + lax.broadcasted_iota(jnp.int32, (count, 1), 0)
        i = q // NOCC
        j = q - i * NOCC
        li = jnp.zeros_like(q)
        lj = jnp.zeros_like(q)
        for n in range(IRREPS - 1):
            start = occ_s[0, n]
            li = li + (i >= start).astype(jnp.int32)
            lj = lj + (j >= start).astype(jnp.int32)
        return jnp.bitwise_xor(li, lj)

    first_label = vir_s[0, 0]

    vir_panel = panel_of(vir, col)
    vir_t = jnp.transpose(jnp.broadcast_to(vir.astype(F32), (128, nvir))).astype(jnp.int32)
    vir_t = jnp.concatenate([vir_t] * (panel // 128), axis=1)
    load_v.wait()
    for c in range(local_c):
        target = jnp.bitwise_xor(vir_panel, jnp.bitwise_xor(first_label, vir_s[0, row * local_c + c]))
        block = integ[c * nvir:(c + 1) * nvir, :]
        masked = jnp.where(vir_t == target, block.astype(F32), 0.0).astype(BF16)
        vbuf[0, c * live:(c + 1) * live, :] = dot(place, masked).astype(BF16)

    pl.semaphore_wait(barrier, rows + cols - 2)

    def send_v(source, slot, device):
        copy = pltpu.make_async_remote_copy(
            src_ref=vbuf.at[source], dst_ref=vbuf.at[slot], send_sem=v_send.at[slot], recv_sem=v_recv.at[slot],
            device_id=device, device_id_type=MESH,
        )
        copy.start()
        return copy

    sibling = (row, chip * 2 + (1 - core))
    v_copies = {}
    for o in range(1, chips):
        v_copies[2 * o] = send_v(0, 2 * o, (row, lax.rem(chip + o, chips) * 2 + core))
    v_copies[1] = send_v(0, 1, sibling)

    own_irrep = pair_irrep((row * cols + col) * pair_rows, pair_rows)
    load_t.wait()
    t_copies = []
    order = [o for o in range(1, rows)] + [0]
    group = 4
    for g in range(0, rows, group):
        offsets = order[g:g + group]
        pieces = []
        for o in offsets:
            peer = lax.rem(row + o, rows)
            for c in range(local_c):
                orbital = peer * local_c + c
                block = amp[:, pl.ds(pl.multiple_of(orbital * nvir, nvir), nvir)]
                hit = vir == jnp.bitwise_xor(own_irrep, vir_s[0, orbital])
                pieces.append(jnp.where(hit, block.astype(F32), 0.0).astype(BF16))
        packed = dot_nt(jnp.concatenate(pieces, axis=0), place).astype(BF16)
        for n, o in enumerate(offsets):
            for c in range(local_c):
                at = (n * local_c + c) * pair_rows
                kept = packed[at:at + pair_rows]
                if o == 0:
                    tbuf[0, :, c * live:(c + 1) * live] = kept
                else:
                    tsend[o - 1, :, c * live:(c + 1) * live] = kept
            if o > 0:
                copy = pltpu.make_async_remote_copy(
                    src_ref=tsend.at[o - 1], dst_ref=tbuf.at[o], send_sem=t_send.at[o], recv_sem=t_recv.at[o],
                    device_id=(lax.rem(row + o, rows), col), device_id_type=MESH,
                )
                copy.start()
                t_copies.append(copy)

    for o in range(1, chips):
        v_copies[2 * o].wait_recv()
        v_copies[2 * o + 1] = send_v(2 * o, 2 * o + 1, sibling)

    irrep_at = []
    for o in range(rows):
        source = lax.rem(row + rows - o, rows)
        irrep_at.append(pair_irrep((source * cols + col) * pair_rows, pair_rows))
    held_irrep = jnp.bitwise_xor(jnp.concatenate(irrep_at, axis=0), first_label)

    for copy in t_copies:
        copy.wait_recv()
    held = jnp.concatenate([tbuf[o] for o in range(rows)], axis=0)
    total = jnp.zeros((rows * pair_rows, live), F32)
    for slot in range(cols):
        if slot % 2 == 1:
            v_copies[slot].wait_recv()
        o, other = slot // 2, slot % 2
        holder = lax.rem(chip + chips - o, chips) * 2 + (core + other * (1 - 2 * core))
        product = dot(held, vbuf[slot])
        product = jnp.where(held_irrep == panel_of(vir, holder), product, 0.0)
        put = placed(panel_of(rank, holder))
        for part in three_parts(product):
            total = total + dot_nt(part, put)

    rpart[...] = total.reshape(rpart.shape)
    r_copies = []
    for o in range(1, rows):
        copy = pltpu.make_async_remote_copy(
            src_ref=rpart.at[o], dst_ref=rrecv.at[o], send_sem=r_send.at[o], recv_sem=r_recv.at[o],
            device_id=(lax.rem(row + rows - o, rows), col), device_id_type=MESH,
        )
        copy.start()
        r_copies.append(copy)

    result = rpart[0]
    for o in range(1, rows):
        r_copies[o - 1].wait_recv()
        result = result + rrecv[o]
    spread = jnp.zeros((pair_rows, nvir), F32)
    for part in three_parts(result):
        spread = spread + dot(part, place)
    out_ref[...] = jnp.where(jnp.bitwise_xor(own_irrep, first_label) == vir, spread, 0.0)

    for copy in list(v_copies.values()) + t_copies + r_copies:
        copy.wait_send()


def body(amplitudes, integrals, vir_irrep, occ_starts, panel_owner):
    rows, cols = lax.axis_size("row"), lax.axis_size("col")
    pair_rows, amp_cols = amplitudes.shape
    slab_rows, panel = integrals.shape
    nvir = vir_irrep.shape[0]
    live = nvir // IRREPS
    kept = (slab_rows // nvir) * live
    anywhere = pl.BlockSpec(memory_space=pl.ANY)
    vector = pl.BlockSpec(memory_space=pltpu.VMEM)
    scalars = pl.BlockSpec(memory_space=pltpu.SMEM)
    dma = pltpu.SemaphoreType.DMA
    return pl.pallas_call(
        functools.partial(kernel, rows, cols, live),
        out_shape=jax.ShapeDtypeStruct((pair_rows, cols * panel), F32),
        in_specs=[anywhere, anywhere, vector, scalars, scalars, scalars],
        out_specs=vector,
        scratch_shapes=[
            pltpu.VMEM((pair_rows, amp_cols), BF16),
            pltpu.VMEM((slab_rows, panel), BF16),
            pltpu.VMEM((rows - 1, pair_rows, kept), BF16),
            pltpu.VMEM((rows, pair_rows, kept), BF16),
            pltpu.VMEM((cols, kept, panel), BF16),
            pltpu.VMEM((rows, pair_rows, live), F32),
            pltpu.VMEM((rows, pair_rows, live), F32),
            dma((2,)),
            dma((rows,)),
            dma((rows,)),
            dma((cols,)),
            dma((cols,)),
            dma((rows,)),
            dma((rows,)),
        ],
        compiler_params=pltpu.CompilerParams(
            collective_id=0, has_side_effects=True, vmem_limit_bytes=48 * 1024 * 1024
        ),
    )(
        amplitudes, integrals, vir_irrep.reshape(1, nvir), vir_irrep.reshape(1, nvir),
        occ_starts.reshape(1, -1), panel_owner,
    )


def solution(mesh):
    in_specs = (P(("row", "col"), None), P("row", "col"), P(), P(), P())
    out_specs = P(("row", "col"), None)
    return jax.shard_map(body, mesh=mesh, in_specs=in_specs, out_specs=out_specs, check_vma=False)
```

```python
import functools

import jax
import jax.numpy as jnp
from jax import lax
from jax.experimental import pallas as pl
from jax.experimental.pallas import tpu as pltpu
from jax.sharding import PartitionSpec as P

IRREPS = 8
NOCC = 120
MESH = pl.DeviceIdType.MESH
F32 = jnp.float32
BF16 = jnp.bfloat16


def dot(a, b):
    return jnp.dot(a, b, preferred_element_type=F32)


def dot_nt(a, b):
    return lax.dot_general(a, b, (((1,), (1,)), ((), ())), preferred_element_type=F32)


def three_parts(x):
    high = x.astype(BF16)
    rest = x - high.astype(F32)
    middle = rest.astype(BF16)
    low = (rest - middle.astype(F32)).astype(BF16)
    return high, middle, low


def remote(source, target, send_sem, recv_sem, device):
    copy = pltpu.make_async_remote_copy(
        src_ref=source, dst_ref=target, send_sem=send_sem, recv_sem=recv_sem,
        device_id=device, device_id_type=MESH,
    )
    copy.start()
    return copy


def kernel(
    rows, cols, live,
    amp_hbm, int_hbm, vir_hbm, occ_hbm, owner_hbm,
    out_ref,
    vir_ref, vir_s, occ_s, owner_s, amp, integ, tsend, tbuf, vbuf, rpart, rrecv,
    load_sem, t_send, t_recv, v_send, v_recv, r_send, r_recv,
):
    row, col = lax.axis_index("row"), lax.axis_index("col")
    pair_rows, amp_cols = amp_hbm.shape
    slab_rows, panel = int_hbm.shape
    nvir = vir_hbm.shape[1]
    local_c = slab_rows // nvir
    chips = cols // 2
    chip, core = col // 2, col % 2

    loads = [
        pltpu.make_async_copy(source, target, load_sem.at[n])
        for n, (source, target) in enumerate((
            (vir_hbm, vir_ref), (vir_hbm, vir_s), (occ_hbm, occ_s), (owner_hbm, owner_s),
            (int_hbm, integ), (amp_hbm, amp),
        ))
    ]
    for load in loads:
        load.start()
    load_v, load_t = loads[-2:]

    barrier = pltpu.get_barrier_semaphore()
    for o in range(1, rows):
        pl.semaphore_signal(barrier, inc=1, device_id=(lax.rem(row + o, rows), col), device_id_type=MESH)
    for o in range(1, cols):
        pl.semaphore_signal(barrier, inc=1, device_id=(row, lax.rem(col + o, cols)), device_id_type=MESH)

    for load in loads[:-2]:
        load.wait()

    vir = vir_ref[...]
    irrep_of = lax.broadcasted_iota(jnp.int32, (IRREPS, nvir), 0)
    onehot = (jnp.broadcast_to(vir, (IRREPS, nvir)) == irrep_of).astype(F32)
    tiles = nvir // 128
    onehot_tiles = [onehot[:, i * 128:(i + 1) * 128] for i in range(tiles)]
    before = (
        lax.broadcasted_iota(jnp.int32, (128, 128), 0) < lax.broadcasted_iota(jnp.int32, (128, 128), 1)
    ).astype(BF16)
    within = dot(jnp.concatenate(onehot_tiles, axis=0).astype(BF16), before)
    carry = jnp.zeros((IRREPS, 1), F32)
    rank_tiles = []
    for i in range(tiles):
        counted = within[i * IRREPS:(i + 1) * IRREPS] + carry
        rank_tiles.append(jnp.sum(onehot_tiles[i] * counted, axis=0, keepdims=True))
        carry = carry + jnp.sum(onehot_tiles[i], axis=1, keepdims=True)
    rank = jnp.concatenate(rank_tiles, axis=1).astype(jnp.int32)

    def placed(row_of_ranks):
        width = row_of_ranks.shape[1]
        return (
            jnp.broadcast_to(row_of_ranks, (live, width)) == lax.broadcasted_iota(jnp.int32, (live, width), 0)
        ).astype(F32).astype(BF16)

    place = placed(rank)

    def panel_of(values, owner):
        result = jnp.zeros((1, panel), jnp.int32)
        for slot in range(cols):
            held = (owner_s[slot, row] == owner).astype(jnp.int32)
            result = result + held * values[:, slot * panel:(slot + 1) * panel]
        return result

    def pair_irrep(first, count):
        q = first + lax.broadcasted_iota(jnp.int32, (count, 1), 0)
        i = q // NOCC
        j = q - i * NOCC
        li = jnp.zeros_like(q)
        lj = jnp.zeros_like(q)
        for n in range(IRREPS - 1):
            start = occ_s[0, n]
            li = li + (i >= start).astype(jnp.int32)
            lj = lj + (j >= start).astype(jnp.int32)
        return jnp.bitwise_xor(li, lj)

    first_label = vir_s[0, 0]

    vir_panel = panel_of(vir, col)
    vir_t = jnp.transpose(jnp.broadcast_to(vir.astype(F32), (128, nvir))).astype(jnp.int32)
    vir_t = jnp.concatenate([vir_t] * (panel // 128), axis=1)
    load_v.wait()
    for c in range(local_c):
        target = jnp.bitwise_xor(vir_panel, jnp.bitwise_xor(first_label, vir_s[0, row * local_c + c]))
        block = integ[c * nvir:(c + 1) * nvir, :]
        masked = jnp.where(vir_t == target, block.astype(F32), 0.0).astype(BF16)
        vbuf[0, c * live:(c + 1) * live, :] = dot(place, masked).astype(BF16)

    pl.semaphore_wait(barrier, rows + cols - 2)

    def send_v(source, slot, device):
        return remote(vbuf.at[source], vbuf.at[slot], v_send.at[slot], v_recv.at[slot], device)

    sibling = (row, chip * 2 + (1 - core))
    v_copies = {}
    for o in range(1, chips):
        v_copies[2 * o] = send_v(0, 2 * o, (row, lax.rem(chip + o, chips) * 2 + core))
    v_copies[1] = send_v(0, 1, sibling)

    own_irrep = pair_irrep((row * cols + col) * pair_rows, pair_rows)
    load_t.wait()
    t_copies = []
    order = [o for o in range(1, rows)] + [0]
    group = 4
    for g in range(0, rows, group):
        offsets = order[g:g + group]
        pieces = []
        for o in offsets:
            peer = lax.rem(row + o, rows)
            for c in range(local_c):
                orbital = peer * local_c + c
                block = amp[:, pl.ds(pl.multiple_of(orbital * nvir, nvir), nvir)]
                hit = vir == jnp.bitwise_xor(own_irrep, vir_s[0, orbital])
                pieces.append(jnp.where(hit, block.astype(F32), 0.0).astype(BF16))
        packed = dot_nt(jnp.concatenate(pieces, axis=0), place).astype(BF16)
        for n, o in enumerate(offsets):
            for c in range(local_c):
                at = (n * local_c + c) * pair_rows
                kept = packed[at:at + pair_rows]
                if o == 0:
                    tbuf[0, :, c * live:(c + 1) * live] = kept
                else:
                    tsend[o - 1, :, c * live:(c + 1) * live] = kept
            if o > 0:
                t_copies.append(remote(
                    tsend.at[o - 1], tbuf.at[o], t_send.at[o], t_recv.at[o], (lax.rem(row + o, rows), col)
                ))

    for o in range(1, chips):
        v_copies[2 * o].wait_recv()
        v_copies[2 * o + 1] = send_v(2 * o, 2 * o + 1, sibling)

    irrep_at = []
    for o in range(rows):
        source = lax.rem(row + rows - o, rows)
        irrep_at.append(pair_irrep((source * cols + col) * pair_rows, pair_rows))
    held_irrep = jnp.bitwise_xor(jnp.concatenate(irrep_at, axis=0), first_label)

    for copy in t_copies:
        copy.wait_recv()
    held = jnp.concatenate([tbuf[o] for o in range(rows)], axis=0)
    total = jnp.zeros((rows * pair_rows, live), F32)
    for slot in range(cols):
        if slot % 2 == 1:
            v_copies[slot].wait_recv()
        o, other = slot // 2, slot % 2
        holder = lax.rem(chip + chips - o, chips) * 2 + (core + other * (1 - 2 * core))
        product = dot(held, vbuf[slot])
        product = jnp.where(held_irrep == panel_of(vir, holder), product, 0.0)
        put = placed(panel_of(rank, holder))
        for part in three_parts(product):
            total = total + dot_nt(part, put)

    rpart[...] = total.reshape(rpart.shape)
    r_copies = []
    for o in range(1, rows):
        r_copies.append(remote(
            rpart.at[o], rrecv.at[o], r_send.at[o], r_recv.at[o], (lax.rem(row + rows - o, rows), col)
        ))

    result = rpart[0]
    for o in range(1, rows):
        r_copies[o - 1].wait_recv()
        result = result + rrecv[o]
    spread = jnp.zeros((pair_rows, nvir), F32)
    for part in three_parts(result):
        spread = spread + dot(part, place)
    out_ref[...] = jnp.where(jnp.bitwise_xor(own_irrep, first_label) == vir, spread, 0.0)

    for copy in list(v_copies.values()) + t_copies + r_copies:
        copy.wait_send()


def body(amplitudes, integrals, vir_irrep, occ_starts, panel_owner):
    rows, cols = lax.axis_size("row"), lax.axis_size("col")
    pair_rows, amp_cols = amplitudes.shape
    slab_rows, panel = integrals.shape
    nvir = vir_irrep.shape[0]
    live = nvir // IRREPS
    kept = (slab_rows // nvir) * live
    anywhere = pl.BlockSpec(memory_space=pl.ANY)
    vector = pl.BlockSpec(memory_space=pltpu.VMEM)
    dma = pltpu.SemaphoreType.DMA
    return pl.pallas_call(
        functools.partial(kernel, rows, cols, live),
        out_shape=jax.ShapeDtypeStruct((pair_rows, cols * panel), F32),
        in_specs=[anywhere] * 5,
        out_specs=vector,
        scratch_shapes=[
            pltpu.VMEM((1, nvir), jnp.int32),
            pltpu.SMEM((1, nvir), jnp.int32),
            pltpu.SMEM((1, IRREPS - 1), jnp.int32),
            pltpu.SMEM((cols, rows), jnp.int32),
            pltpu.VMEM((pair_rows, amp_cols), BF16),
            pltpu.VMEM((slab_rows, panel), BF16),
            pltpu.VMEM((rows - 1, pair_rows, kept), BF16),
            pltpu.VMEM((rows, pair_rows, kept), BF16),
            pltpu.VMEM((cols, kept, panel), BF16),
            pltpu.VMEM((rows, pair_rows, live), F32),
            pltpu.VMEM((rows, pair_rows, live), F32),
            dma((6,)),
            dma((rows,)),
            dma((rows,)),
            dma((cols,)),
            dma((cols,)),
            dma((rows,)),
            dma((rows,)),
        ],
        compiler_params=pltpu.CompilerParams(
            collective_id=0, has_side_effects=True, vmem_limit_bytes=62 * 1024 * 1024
        ),
    )(
        amplitudes, integrals, vir_irrep.reshape(1, nvir), occ_starts.reshape(1, -1), panel_owner.T,
    )


def solution(mesh):
    in_specs = (P(("row", "col"), None), P("row", "col"), P(), P(), P())
    out_specs = P(("row", "col"), None)
    return jax.shard_map(body, mesh=mesh, in_specs=in_specs, out_specs=out_specs, check_vma=False)
```

```python
import functools

import jax
import jax.numpy as jnp
from jax import lax
from jax.experimental import pallas as pl
from jax.experimental.pallas import tpu as pltpu
from jax.sharding import PartitionSpec as P

IRREPS = 8
NOCC = 120
MESH = pl.DeviceIdType.MESH
F32 = jnp.float32
BF16 = jnp.bfloat16


def dot(a, b):
    return jnp.dot(a, b, preferred_element_type=F32)


def dot_nt(a, b):
    return lax.dot_general(a, b, (((1,), (1,)), ((), ())), preferred_element_type=F32)


def three_parts(x):
    high = x.astype(BF16)
    rest = x - high.astype(F32)
    middle = rest.astype(BF16)
    low = (rest - middle.astype(F32)).astype(BF16)
    return high, middle, low


def remote(source, target, send_sem, recv_sem, device):
    copy = pltpu.make_async_remote_copy(
        src_ref=source, dst_ref=target, send_sem=send_sem, recv_sem=recv_sem,
        device_id=device, device_id_type=MESH,
    )
    copy.start()
    return copy


def kernel(
    rows, cols, live,
    amp_hbm, int_hbm, vir_hbm, occ_hbm, owner_hbm,
    out_ref,
    vir_ref, vir_s, occ_s, owner_s, amp, integ, tsend, tbuf, vbuf, rpart, rrecv,
    load_sem, t_send, t_recv, v_send, v_recv, r_send, r_recv,
):
    row, col = lax.axis_index("row"), lax.axis_index("col")
    pair_rows, amp_cols = amp_hbm.shape
    slab_rows, panel = int_hbm.shape
    nvir = vir_hbm.shape[1]
    local_c = slab_rows // nvir
    chips = cols // 2
    chip, core = col // 2, col % 2

    order = [o for o in range(1, rows)] + [0]
    wide = local_c * nvir
    pairs = [(vir_hbm, vir_ref), (vir_hbm, vir_s), (occ_hbm, occ_s), (owner_hbm, owner_s)]
    small = len(pairs)
    for c in range(local_c):
        strip = pl.ds(c * nvir, nvir)
        pairs.append((int_hbm.at[strip], integ.at[strip]))
    for o in order:
        strip = pl.ds(pl.multiple_of(lax.rem(row + o, rows) * wide, wide), wide)
        pairs.append((amp_hbm.at[:, strip], amp.at[o]))
    loads = [pltpu.make_async_copy(source, target, load_sem.at[n]) for n, (source, target) in enumerate(pairs)]
    for load in loads:
        load.start()
    load_v = loads[small:small + local_c]
    load_t = dict(zip(order, loads[small + local_c:]))

    barrier = pltpu.get_barrier_semaphore()
    for o in range(1, rows):
        pl.semaphore_signal(barrier, inc=1, device_id=(lax.rem(row + o, rows), col), device_id_type=MESH)
    for o in range(1, cols):
        pl.semaphore_signal(barrier, inc=1, device_id=(row, lax.rem(col + o, cols)), device_id_type=MESH)

    for load in loads[:small]:
        load.wait()

    vir = vir_ref[...]
    irrep_of = lax.broadcasted_iota(jnp.int32, (IRREPS, nvir), 0)
    onehot = (jnp.broadcast_to(vir, (IRREPS, nvir)) == irrep_of).astype(F32)
    tiles = nvir // 128
    onehot_tiles = [onehot[:, i * 128:(i + 1) * 128] for i in range(tiles)]
    before = (
        lax.broadcasted_iota(jnp.int32, (128, 128), 0) < lax.broadcasted_iota(jnp.int32, (128, 128), 1)
    ).astype(BF16)
    within = dot(jnp.concatenate(onehot_tiles, axis=0).astype(BF16), before)
    carry = jnp.zeros((IRREPS, 1), F32)
    rank_tiles = []
    for i in range(tiles):
        counted = within[i * IRREPS:(i + 1) * IRREPS] + carry
        rank_tiles.append(jnp.sum(onehot_tiles[i] * counted, axis=0, keepdims=True))
        carry = carry + jnp.sum(onehot_tiles[i], axis=1, keepdims=True)
    rank = jnp.concatenate(rank_tiles, axis=1).astype(jnp.int32)

    def placed(row_of_ranks):
        width = row_of_ranks.shape[1]
        return (
            jnp.broadcast_to(row_of_ranks, (live, width)) == lax.broadcasted_iota(jnp.int32, (live, width), 0)
        ).astype(F32).astype(BF16)

    place = placed(rank)

    def panel_of(values, owner):
        result = jnp.zeros((1, panel), jnp.int32)
        for slot in range(cols):
            held = (owner_s[slot, row] == owner).astype(jnp.int32)
            result = result + held * values[:, slot * panel:(slot + 1) * panel]
        return result

    def pair_irrep(first, count):
        q = first + lax.broadcasted_iota(jnp.int32, (count, 1), 0)
        i = q // NOCC
        j = q - i * NOCC
        li = jnp.zeros_like(q)
        lj = jnp.zeros_like(q)
        for n in range(IRREPS - 1):
            start = occ_s[0, n]
            li = li + (i >= start).astype(jnp.int32)
            lj = lj + (j >= start).astype(jnp.int32)
        return jnp.bitwise_xor(li, lj)

    first_label = vir_s[0, 0]

    vir_panel = panel_of(vir, col)
    vir_t = jnp.transpose(jnp.broadcast_to(vir.astype(F32), (128, nvir))).astype(jnp.int32)
    vir_t = jnp.concatenate([vir_t] * (panel // 128), axis=1)
    for c in range(local_c):
        load_v[c].wait()
        target = jnp.bitwise_xor(vir_panel, jnp.bitwise_xor(first_label, vir_s[0, row * local_c + c]))
        block = integ[c * nvir:(c + 1) * nvir, :]
        masked = jnp.where(vir_t == target, block.astype(F32), 0.0).astype(BF16)
        vbuf[0, c * live:(c + 1) * live, :] = dot(place, masked).astype(BF16)

    pl.semaphore_wait(barrier, rows + cols - 2)

    def send_v(source, slot, c, device):
        strip = pl.ds(c * live, live)
        return remote(
            vbuf.at[source, strip], vbuf.at[slot, strip], v_send.at[slot, c], v_recv.at[slot, c], device
        )

    sibling = (row, chip * 2 + (1 - core))
    v_copies = {}
    for c in range(local_c):
        for o in range(1, chips):
            v_copies[2 * o, c] = send_v(0, 2 * o, c, (row, lax.rem(chip + o, chips) * 2 + core))
        v_copies[1, c] = send_v(0, 1, c, sibling)

    own_irrep = pair_irrep((row * cols + col) * pair_rows, pair_rows)
    t_copies = {}
    group = 2
    for g in range(0, rows, group):
        offsets = order[g:g + group]
        pieces = []
        for o in offsets:
            peer = lax.rem(row + o, rows)
            load_t[o].wait()
            for c in range(local_c):
                orbital = peer * local_c + c
                block = amp[o, :, c * nvir:(c + 1) * nvir]
                hit = vir == jnp.bitwise_xor(own_irrep, vir_s[0, orbital])
                pieces.append(jnp.where(hit, block.astype(F32), 0.0).astype(BF16))
        packed = dot_nt(jnp.concatenate(pieces, axis=0), place).astype(BF16)
        for n, o in enumerate(offsets):
            for c in range(local_c):
                at = (n * local_c + c) * pair_rows
                kept = packed[at:at + pair_rows]
                if o == 0:
                    tbuf[0, :, c * live:(c + 1) * live] = kept
                else:
                    tsend[o - 1, :, c * live:(c + 1) * live] = kept
            if o > 0:
                t_copies[o] = remote(
                    tsend.at[o - 1], tbuf.at[o], t_send.at[o], t_recv.at[o], (lax.rem(row + o, rows), col)
                )

    for c in range(local_c):
        for o in range(1, chips):
            v_copies[2 * o, c].wait_recv()
            v_copies[2 * o + 1, c] = send_v(2 * o, 2 * o + 1, c, sibling)

    irrep_at = []
    for o in range(rows):
        source = lax.rem(row + rows - o, rows)
        irrep_at.append(pair_irrep((source * cols + col) * pair_rows, pair_rows))
    held_irrep = jnp.bitwise_xor(jnp.concatenate(irrep_at, axis=0), first_label)

    panel_irrep, panel_place = [], []
    for slot in range(cols):
        o, other = slot // 2, slot % 2
        holder = lax.rem(chip + chips - o, chips) * 2 + (core + other * (1 - 2 * core))
        panel_irrep.append(panel_of(vir, holder))
        panel_place.append(placed(panel_of(rank, holder)))
    r_copies = []
    half = rows // 2
    for first in range(0, rows, half):
        offsets = range(first, first + half)
        for o in offsets:
            if o > 0:
                t_copies[o].wait_recv()
        span = slice(first * pair_rows, (first + half) * pair_rows)
        held = jnp.concatenate([tbuf[o] for o in offsets], axis=0)
        total = jnp.zeros((half * pair_rows, live), F32)
        for slot in range(cols):
            if slot % 2 == 1 and first == 0:
                for c in range(local_c):
                    v_copies[slot, c].wait_recv()
            product = dot(held, vbuf[slot])
            product = jnp.where(held_irrep[span] == panel_irrep[slot], product, 0.0)
            for part in three_parts(product):
                total = total + dot_nt(part, panel_place[slot])
        for n, o in enumerate(offsets):
            rpart[o] = total[n * pair_rows:(n + 1) * pair_rows]
            if o > 0:
                r_copies.append(remote(
                    rpart.at[o], rrecv.at[o], r_send.at[o], r_recv.at[o], (lax.rem(row + rows - o, rows), col)
                ))

    result = rpart[0]
    for o in range(1, rows):
        r_copies[o - 1].wait_recv()
        result = result + rrecv[o]
    spread = jnp.zeros((pair_rows, nvir), F32)
    for part in three_parts(result):
        spread = spread + dot(part, place)
    out_ref[...] = jnp.where(jnp.bitwise_xor(own_irrep, first_label) == vir, spread, 0.0)

    for copy in list(v_copies.values()) + list(t_copies.values()) + r_copies:
        copy.wait_send()


def body(amplitudes, integrals, vir_irrep, occ_starts, panel_owner):
    rows, cols = lax.axis_size("row"), lax.axis_size("col")
    pair_rows, amp_cols = amplitudes.shape
    slab_rows, panel = integrals.shape
    nvir = vir_irrep.shape[0]
    live = nvir // IRREPS
    kept = (slab_rows // nvir) * live
    anywhere = pl.BlockSpec(memory_space=pl.ANY)
    vector = pl.BlockSpec(memory_space=pltpu.VMEM)
    dma = pltpu.SemaphoreType.DMA
    return pl.pallas_call(
        functools.partial(kernel, rows, cols, live),
        out_shape=jax.ShapeDtypeStruct((pair_rows, cols * panel), F32),
        in_specs=[anywhere] * 5,
        out_specs=vector,
        scratch_shapes=[
            pltpu.VMEM((1, nvir), jnp.int32),
            pltpu.SMEM((1, nvir), jnp.int32),
            pltpu.SMEM((1, IRREPS - 1), jnp.int32),
            pltpu.SMEM((cols, rows), jnp.int32),
            pltpu.VMEM((rows, pair_rows, amp_cols // rows), BF16),
            pltpu.VMEM((slab_rows, panel), BF16),
            pltpu.VMEM((rows - 1, pair_rows, kept), BF16),
            pltpu.VMEM((rows, pair_rows, kept), BF16),
            pltpu.VMEM((cols, kept, panel), BF16),
            pltpu.VMEM((rows, pair_rows, live), F32),
            pltpu.VMEM((rows, pair_rows, live), F32),
            dma((4 + slab_rows // nvir + rows,)),
            dma((rows,)),
            dma((rows,)),
            dma((cols, slab_rows // nvir)),
            dma((cols, slab_rows // nvir)),
            dma((rows,)),
            dma((rows,)),
        ],
        compiler_params=pltpu.CompilerParams(
            collective_id=0, has_side_effects=True, vmem_limit_bytes=62 * 1024 * 1024
        ),
    )(
        amplitudes, integrals, vir_irrep.reshape(1, nvir), occ_starts.reshape(1, -1), panel_owner.T,
    )


def solution(mesh):
    in_specs = (P(("row", "col"), None), P("row", "col"), P(), P(), P())
    out_specs = P(("row", "col"), None)
    return jax.shard_map(body, mesh=mesh, in_specs=in_specs, out_specs=out_specs, check_vma=False)
```

```python
import functools

import jax
import jax.numpy as jnp
from jax import lax
from jax.experimental import pallas as pl
from jax.experimental.pallas import tpu as pltpu
from jax.sharding import PartitionSpec as P

IRREPS = 8
NOCC = 120
MESH = pl.DeviceIdType.MESH
F32 = jnp.float32
BF16 = jnp.bfloat16


def dot(a, b):
    return jnp.dot(a, b, preferred_element_type=F32)


def dot_nt(a, b):
    return lax.dot_general(a, b, (((1,), (1,)), ((), ())), preferred_element_type=F32)


def three_parts(x):
    high = x.astype(BF16)
    rest = x - high.astype(F32)
    middle = rest.astype(BF16)
    low = (rest - middle.astype(F32)).astype(BF16)
    return high, middle, low


def remote(source, target, send_sem, recv_sem, device):
    copy = pltpu.make_async_remote_copy(
        src_ref=source, dst_ref=target, send_sem=send_sem, recv_sem=recv_sem,
        device_id=device, device_id_type=MESH,
    )
    copy.start()
    return copy


def kernel(
    rows, cols, live,
    amp_hbm, int_hbm, vir_hbm, occ_hbm, owner_hbm,
    out_ref,
    vir_ref, vir_s, occ_s, owner_s, amp, integ, tsend, tbuf, vbuf, rpart, rrecv,
    load_sem, t_send, t_recv, v_send, v_recv, r_send, r_recv,
):
    row, col = lax.axis_index("row"), lax.axis_index("col")
    pair_rows, amp_cols = amp_hbm.shape
    slab_rows, panel = int_hbm.shape
    nvir = vir_hbm.shape[1]
    local_c = slab_rows // nvir
    chips = cols // 2
    chip, core = col // 2, col % 2

    order = [o for o in range(1, rows)] + [0]
    wide = local_c * nvir
    pairs = [(vir_hbm, vir_ref), (vir_hbm, vir_s), (occ_hbm, occ_s), (owner_hbm, owner_s)]
    small = len(pairs)
    for c in range(local_c):
        strip = pl.ds(c * nvir, nvir)
        pairs.append((int_hbm.at[strip], integ.at[strip]))
    for o in order:
        strip = pl.ds(pl.multiple_of(lax.rem(row + o, rows) * wide, wide), wide)
        pairs.append((amp_hbm.at[:, strip], amp.at[o]))
    loads = [pltpu.make_async_copy(source, target, load_sem.at[n]) for n, (source, target) in enumerate(pairs)]
    for load in loads:
        load.start()
    load_v = loads[small:small + local_c]
    load_t = dict(zip(order, loads[small + local_c:]))

    barrier = pltpu.get_barrier_semaphore()
    for o in range(1, rows):
        pl.semaphore_signal(barrier, inc=1, device_id=(lax.rem(row + o, rows), col), device_id_type=MESH)
    for o in range(1, cols):
        pl.semaphore_signal(barrier, inc=1, device_id=(row, lax.rem(col + o, cols)), device_id_type=MESH)

    for load in loads[:small]:
        load.wait()

    vir = vir_ref[...]
    irrep_of = lax.broadcasted_iota(jnp.int32, (IRREPS, nvir), 0)
    onehot = (jnp.broadcast_to(vir, (IRREPS, nvir)) == irrep_of).astype(F32)
    tiles = nvir // 128
    onehot_tiles = [onehot[:, i * 128:(i + 1) * 128] for i in range(tiles)]
    before = (
        lax.broadcasted_iota(jnp.int32, (128, 128), 0) < lax.broadcasted_iota(jnp.int32, (128, 128), 1)
    ).astype(BF16)
    within = dot(jnp.concatenate(onehot_tiles, axis=0).astype(BF16), before)
    carry = jnp.zeros((IRREPS, 1), F32)
    rank_tiles = []
    for i in range(tiles):
        counted = within[i * IRREPS:(i + 1) * IRREPS] + carry
        rank_tiles.append(jnp.sum(onehot_tiles[i] * counted, axis=0, keepdims=True))
        carry = carry + jnp.sum(onehot_tiles[i], axis=1, keepdims=True)
    rank = jnp.concatenate(rank_tiles, axis=1).astype(jnp.int32)

    def placed(row_of_ranks):
        width = row_of_ranks.shape[1]
        return (
            jnp.broadcast_to(row_of_ranks, (live, width)) == lax.broadcasted_iota(jnp.int32, (live, width), 0)
        ).astype(F32).astype(BF16)

    place = placed(rank)

    def panel_of(values, owner):
        result = jnp.zeros((1, panel), jnp.int32)
        for slot in range(cols):
            held = (owner_s[slot, row] == owner).astype(jnp.int32)
            result = result + held * values[:, slot * panel:(slot + 1) * panel]
        return result

    def pair_irrep(first, count):
        q = first + lax.broadcasted_iota(jnp.int32, (count, 1), 0)
        i = q // NOCC
        j = q - i * NOCC
        li = jnp.zeros_like(q)
        lj = jnp.zeros_like(q)
        for n in range(IRREPS - 1):
            start = occ_s[0, n]
            li = li + (i >= start).astype(jnp.int32)
            lj = lj + (j >= start).astype(jnp.int32)
        return jnp.bitwise_xor(li, lj)

    first_label = vir_s[0, 0]

    def send_v(source, slot, c, device):
        strip = pl.ds(c * live, live)
        return remote(
            vbuf.at[source, strip], vbuf.at[slot, strip], v_send.at[slot, c], v_recv.at[slot, c], device
        )

    sibling = (row, chip * 2 + (1 - core))
    v_copies = {}
    vir_panel = panel_of(vir, col)
    vir_t = jnp.transpose(jnp.broadcast_to(vir.astype(F32), (128, nvir))).astype(jnp.int32)
    vir_t = jnp.concatenate([vir_t] * (panel // 128), axis=1)
    for c in range(local_c):
        load_v[c].wait()
        target = jnp.bitwise_xor(vir_panel, jnp.bitwise_xor(first_label, vir_s[0, row * local_c + c]))
        block = integ[c * nvir:(c + 1) * nvir, :]
        masked = jnp.where(vir_t == target, block.astype(F32), 0.0).astype(BF16)
        vbuf[0, c * live:(c + 1) * live, :] = dot(place, masked).astype(BF16)
        if c == 0:
            pl.semaphore_wait(barrier, rows + cols - 2)
        for o in range(1, chips):
            v_copies[2 * o, c] = send_v(0, 2 * o, c, (row, lax.rem(chip + o, chips) * 2 + core))
        v_copies[1, c] = send_v(0, 1, c, sibling)

    own_irrep = pair_irrep((row * cols + col) * pair_rows, pair_rows)
    t_copies = {}
    group = 2
    for g in range(0, rows, group):
        offsets = order[g:g + group]
        pieces = []
        for o in offsets:
            peer = lax.rem(row + o, rows)
            load_t[o].wait()
            for c in range(local_c):
                orbital = peer * local_c + c
                block = amp[o, :, c * nvir:(c + 1) * nvir]
                hit = vir == jnp.bitwise_xor(own_irrep, vir_s[0, orbital])
                pieces.append(jnp.where(hit, block.astype(F32), 0.0).astype(BF16))
        packed = dot_nt(jnp.concatenate(pieces, axis=0), place).astype(BF16)
        for n, o in enumerate(offsets):
            for c in range(local_c):
                at = (n * local_c + c) * pair_rows
                kept = packed[at:at + pair_rows]
                if o == 0:
                    tbuf[0, :, c * live:(c + 1) * live] = kept
                else:
                    tsend[o - 1, :, c * live:(c + 1) * live] = kept
            if o > 0:
                t_copies[o] = remote(
                    tsend.at[o - 1], tbuf.at[o], t_send.at[o], t_recv.at[o], (lax.rem(row + o, rows), col)
                )

    for c in range(local_c):
        for o in range(1, chips):
            v_copies[2 * o, c].wait_recv()
            v_copies[2 * o + 1, c] = send_v(2 * o, 2 * o + 1, c, sibling)

    irrep_at = []
    for o in range(rows):
        source = lax.rem(row + rows - o, rows)
        irrep_at.append(pair_irrep((source * cols + col) * pair_rows, pair_rows))
    held_irrep = jnp.bitwise_xor(jnp.concatenate(irrep_at, axis=0), first_label)

    panel_irrep, panel_place = [], []
    for slot in range(cols):
        o, other = slot // 2, slot % 2
        holder = lax.rem(chip + chips - o, chips) * 2 + (core + other * (1 - 2 * core))
        panel_irrep.append(panel_of(vir, holder))
        panel_place.append(placed(panel_of(rank, holder)))
    r_copies = []
    half = rows // 2
    for first in range(0, rows, half):
        offsets = range(first, first + half)
        for o in offsets:
            if o > 0:
                t_copies[o].wait_recv()
        span = slice(first * pair_rows, (first + half) * pair_rows)
        held = jnp.concatenate([tbuf[o] for o in offsets], axis=0)
        total = jnp.zeros((half * pair_rows, live), F32)
        for slot in range(cols):
            if slot % 2 == 1 and first == 0:
                for c in range(local_c):
                    v_copies[slot, c].wait_recv()
            product = dot(held, vbuf[slot])
            product = jnp.where(held_irrep[span] == panel_irrep[slot], product, 0.0)
            for part in three_parts(product):
                total = total + dot_nt(part, panel_place[slot])
        for n, o in enumerate(offsets):
            rpart[o] = total[n * pair_rows:(n + 1) * pair_rows]
            if o > 0:
                r_copies.append(remote(
                    rpart.at[o], rrecv.at[o], r_send.at[o], r_recv.at[o], (lax.rem(row + rows - o, rows), col)
                ))

    result = rpart[0]
    for o in range(1, rows):
        r_copies[o - 1].wait_recv()
        result = result + rrecv[o]
    spread = jnp.zeros((pair_rows, nvir), F32)
    for part in three_parts(result):
        spread = spread + dot(part, place)
    out_ref[...] = jnp.where(jnp.bitwise_xor(own_irrep, first_label) == vir, spread, 0.0)

    for copy in list(v_copies.values()) + list(t_copies.values()) + r_copies:
        copy.wait_send()


def body(amplitudes, integrals, vir_irrep, occ_starts, panel_owner):
    rows, cols = lax.axis_size("row"), lax.axis_size("col")
    pair_rows, amp_cols = amplitudes.shape
    slab_rows, panel = integrals.shape
    nvir = vir_irrep.shape[0]
    live = nvir // IRREPS
    kept = (slab_rows // nvir) * live
    anywhere = pl.BlockSpec(memory_space=pl.ANY)
    vector = pl.BlockSpec(memory_space=pltpu.VMEM)
    dma = pltpu.SemaphoreType.DMA
    return pl.pallas_call(
        functools.partial(kernel, rows, cols, live),
        out_shape=jax.ShapeDtypeStruct((pair_rows, cols * panel), F32),
        in_specs=[anywhere] * 5,
        out_specs=vector,
        scratch_shapes=[
            pltpu.VMEM((1, nvir), jnp.int32),
            pltpu.SMEM((1, nvir), jnp.int32),
            pltpu.SMEM((1, IRREPS - 1), jnp.int32),
            pltpu.SMEM((cols, rows), jnp.int32),
            pltpu.VMEM((rows, pair_rows, amp_cols // rows), BF16),
            pltpu.VMEM((slab_rows, panel), BF16),
            pltpu.VMEM((rows - 1, pair_rows, kept), BF16),
            pltpu.VMEM((rows, pair_rows, kept), BF16),
            pltpu.VMEM((cols, kept, panel), BF16),
            pltpu.VMEM((rows, pair_rows, live), F32),
            pltpu.VMEM((rows, pair_rows, live), F32),
            dma((4 + slab_rows // nvir + rows,)),
            dma((rows,)),
            dma((rows,)),
            dma((cols, slab_rows // nvir)),
            dma((cols, slab_rows // nvir)),
            dma((rows,)),
            dma((rows,)),
        ],
        compiler_params=pltpu.CompilerParams(
            collective_id=0, has_side_effects=True, vmem_limit_bytes=62 * 1024 * 1024
        ),
    )(
        amplitudes, integrals, vir_irrep.reshape(1, nvir), occ_starts.reshape(1, -1), panel_owner.T,
    )


def solution(mesh):
    in_specs = (P(("row", "col"), None), P("row", "col"), P(), P(), P())
    out_specs = P(("row", "col"), None)
    return jax.shard_map(body, mesh=mesh, in_specs=in_specs, out_specs=out_specs, check_vma=False)
```

```python
import functools

import jax
import jax.numpy as jnp
from jax import lax
from jax.experimental import pallas as pl
from jax.experimental.pallas import tpu as pltpu
from jax.sharding import PartitionSpec as P

IRREPS = 8
NOCC = 120
MESH = pl.DeviceIdType.MESH
F32 = jnp.float32
BF16 = jnp.bfloat16


def dot(a, b):
    return jnp.dot(a, b, preferred_element_type=F32)


def dot_nt(a, b):
    return lax.dot_general(a, b, (((1,), (1,)), ((), ())), preferred_element_type=F32)


def three_parts(x):
    high = x.astype(BF16)
    rest = x - high.astype(F32)
    middle = rest.astype(BF16)
    low = (rest - middle.astype(F32)).astype(BF16)
    return high, middle, low


def remote(source, target, send_sem, recv_sem, device):
    copy = pltpu.make_async_remote_copy(
        src_ref=source, dst_ref=target, send_sem=send_sem, recv_sem=recv_sem,
        device_id=device, device_id_type=MESH,
    )
    copy.start()
    return copy


def kernel(
    rows, cols, live,
    amp_hbm, int_hbm, vir_hbm, occ_hbm, owner_hbm,
    out_ref,
    vir_ref, vir_s, occ_s, owner_s, amp, integ, tsend, tbuf, vbuf, rpart, rrecv,
    load_sem, t_send, t_recv, v_send, v_recv, r_send, r_recv,
):
    row, col = lax.axis_index("row"), lax.axis_index("col")
    pair_rows, amp_cols = amp_hbm.shape
    slab_rows, panel = int_hbm.shape
    nvir = vir_hbm.shape[1]
    local_c = slab_rows // nvir
    chips = cols // 2
    chip, core = col // 2, col % 2

    order = [o for o in range(1, rows)] + [0]
    wide = local_c * nvir
    pairs = [(vir_hbm, vir_ref), (vir_hbm, vir_s), (occ_hbm, occ_s), (owner_hbm, owner_s)]
    small = len(pairs)
    for c in range(local_c):
        strip = pl.ds(c * nvir, nvir)
        pairs.append((int_hbm.at[strip], integ.at[strip]))
    for o in order:
        strip = pl.ds(pl.multiple_of(lax.rem(row + o, rows) * wide, wide), wide)
        pairs.append((amp_hbm.at[:, strip], amp.at[o]))
    loads = [pltpu.make_async_copy(source, target, load_sem.at[n]) for n, (source, target) in enumerate(pairs)]
    for load in loads:
        load.start()
    load_v = loads[small:small + local_c]
    load_t = dict(zip(order, loads[small + local_c:]))

    barrier = pltpu.get_barrier_semaphore()
    for o in range(1, rows):
        pl.semaphore_signal(barrier, inc=1, device_id=(lax.rem(row + o, rows), col), device_id_type=MESH)
    for o in range(1, cols):
        pl.semaphore_signal(barrier, inc=1, device_id=(row, lax.rem(col + o, cols)), device_id_type=MESH)

    for load in loads[:small]:
        load.wait()

    vir = vir_ref[...]
    irrep_of = lax.broadcasted_iota(jnp.int32, (IRREPS, nvir), 0)
    onehot = (jnp.broadcast_to(vir, (IRREPS, nvir)) == irrep_of).astype(F32)
    tiles = nvir // 128
    onehot_tiles = [onehot[:, i * 128:(i + 1) * 128] for i in range(tiles)]
    before = (
        lax.broadcasted_iota(jnp.int32, (128, 128), 0) < lax.broadcasted_iota(jnp.int32, (128, 128), 1)
    ).astype(BF16)
    within = dot(jnp.concatenate(onehot_tiles, axis=0).astype(BF16), before)
    carry = jnp.zeros((IRREPS, 1), F32)
    rank_tiles = []
    for i in range(tiles):
        counted = within[i * IRREPS:(i + 1) * IRREPS] + carry
        rank_tiles.append(jnp.sum(onehot_tiles[i] * counted, axis=0, keepdims=True))
        carry = carry + jnp.sum(onehot_tiles[i], axis=1, keepdims=True)
    rank = jnp.concatenate(rank_tiles, axis=1).astype(jnp.int32)

    def placed(row_of_ranks):
        width = row_of_ranks.shape[1]
        return (
            jnp.broadcast_to(row_of_ranks, (live, width)) == lax.broadcasted_iota(jnp.int32, (live, width), 0)
        ).astype(F32).astype(BF16)

    place = placed(rank)

    def panel_of(values, owner):
        result = jnp.zeros((1, panel), jnp.int32)
        for slot in range(cols):
            held = (owner_s[slot, row] == owner).astype(jnp.int32)
            result = result + held * values[:, slot * panel:(slot + 1) * panel]
        return result

    def pair_irrep(first, count):
        q = first + lax.broadcasted_iota(jnp.int32, (count, 1), 0)
        i = q // NOCC
        j = q - i * NOCC
        li = jnp.zeros_like(q)
        lj = jnp.zeros_like(q)
        for n in range(IRREPS - 1):
            start = occ_s[0, n]
            li = li + (i >= start).astype(jnp.int32)
            lj = lj + (j >= start).astype(jnp.int32)
        return jnp.bitwise_xor(li, lj)

    first_label = vir_s[0, 0]

    def send_v(source, slot, c, device):
        strip = pl.ds(c * live, live)
        return remote(
            vbuf.at[source, strip], vbuf.at[slot, strip], v_send.at[slot, c], v_recv.at[slot, c], device
        )

    sibling = (row, chip * 2 + (1 - core))
    v_copies = {}
    vir_panel = panel_of(vir, col)
    vir_t = jnp.transpose(jnp.broadcast_to(vir.astype(F32), (128, nvir))).astype(jnp.int32)
    vir_t = jnp.concatenate([vir_t] * (panel // 128), axis=1)
    for c in range(local_c):
        load_v[c].wait()
        target = jnp.bitwise_xor(vir_panel, jnp.bitwise_xor(first_label, vir_s[0, row * local_c + c]))
        block = integ[c * nvir:(c + 1) * nvir, :]
        masked = jnp.where(vir_t == target, block.astype(F32), 0.0).astype(BF16)
        vbuf[0, c * live:(c + 1) * live, :] = dot(place, masked).astype(BF16)
        if c == 0:
            pl.semaphore_wait(barrier, rows + cols - 2)
        for o in range(1, chips):
            v_copies[2 * o, c] = send_v(0, 2 * o, c, (row, lax.rem(chip + o, chips) * 2 + core))
        v_copies[1, c] = send_v(0, 1, c, sibling)

    own_irrep = pair_irrep((row * cols + col) * pair_rows, pair_rows)
    t_copies = {}
    group = 2
    for g in range(0, rows, group):
        offsets = order[g:g + group]
        pieces = []
        for o in offsets:
            peer = lax.rem(row + o, rows)
            load_t[o].wait()
            for c in range(local_c):
                orbital = peer * local_c + c
                block = amp[o, :, c * nvir:(c + 1) * nvir]
                hit = vir == jnp.bitwise_xor(own_irrep, vir_s[0, orbital])
                pieces.append(jnp.where(hit, block.astype(F32), 0.0).astype(BF16))
        packed = dot_nt(jnp.concatenate(pieces, axis=0), place).astype(BF16)
        for n, o in enumerate(offsets):
            for c in range(local_c):
                at = (n * local_c + c) * pair_rows
                kept = packed[at:at + pair_rows]
                if o == 0:
                    tbuf[0, :, c * live:(c + 1) * live] = kept
                else:
                    tsend[o - 1, :, c * live:(c + 1) * live] = kept
            if o > 0:
                t_copies[o] = remote(
                    tsend.at[o - 1], tbuf.at[o], t_send.at[o], t_recv.at[o], (lax.rem(row + o, rows), col)
                )

    irrep_at = []
    for o in range(rows):
        source = lax.rem(row + rows - o, rows)
        irrep_at.append(pair_irrep((source * cols + col) * pair_rows, pair_rows))
    held_irrep = jnp.bitwise_xor(jnp.concatenate(irrep_at, axis=0), first_label)

    panel_irrep, panel_place = [], []
    for slot in range(cols):
        o, other = slot // 2, slot % 2
        holder = lax.rem(chip + chips - o, chips) * 2 + (core + other * (1 - 2 * core))
        panel_irrep.append(panel_of(vir, holder))
        panel_place.append(placed(panel_of(rank, holder)))

    for c in range(local_c):
        for o in range(1, chips):
            v_copies[2 * o, c].wait_recv()
            v_copies[2 * o + 1, c] = send_v(2 * o, 2 * o + 1, c, sibling)

    r_copies = []
    half = rows // 2
    for first in range(0, rows, half):
        offsets = range(first, first + half)
        for o in offsets:
            if o > 0:
                t_copies[o].wait_recv()
        span = slice(first * pair_rows, (first + half) * pair_rows)
        held = jnp.concatenate([tbuf[o] for o in offsets], axis=0)
        total = jnp.zeros((half * pair_rows, live), F32)
        for slot in range(cols):
            if slot % 2 == 1 and first == 0:
                for c in range(local_c):
                    v_copies[slot, c].wait_recv()
            product = dot(held, vbuf[slot])
            product = jnp.where(held_irrep[span] == panel_irrep[slot], product, 0.0)
            for part in three_parts(product):
                total = total + dot_nt(part, panel_place[slot])
        for n, o in enumerate(offsets):
            rpart[o] = total[n * pair_rows:(n + 1) * pair_rows]
            if o > 0:
                r_copies.append(remote(
                    rpart.at[o], rrecv.at[o], r_send.at[o], r_recv.at[o], (lax.rem(row + rows - o, rows), col)
                ))

    result = rpart[0]
    for o in range(1, rows):
        r_copies[o - 1].wait_recv()
        result = result + rrecv[o]
    spread = jnp.zeros((pair_rows, nvir), F32)
    for part in three_parts(result):
        spread = spread + dot(part, place)
    out_ref[...] = jnp.where(jnp.bitwise_xor(own_irrep, first_label) == vir, spread, 0.0)

    for copy in list(v_copies.values()) + list(t_copies.values()) + r_copies:
        copy.wait_send()


def body(amplitudes, integrals, vir_irrep, occ_starts, panel_owner):
    rows, cols = lax.axis_size("row"), lax.axis_size("col")
    pair_rows, amp_cols = amplitudes.shape
    slab_rows, panel = integrals.shape
    nvir = vir_irrep.shape[0]
    live = nvir // IRREPS
    kept = (slab_rows // nvir) * live
    anywhere = pl.BlockSpec(memory_space=pl.ANY)
    vector = pl.BlockSpec(memory_space=pltpu.VMEM)
    dma = pltpu.SemaphoreType.DMA
    return pl.pallas_call(
        functools.partial(kernel, rows, cols, live),
        out_shape=jax.ShapeDtypeStruct((pair_rows, cols * panel), F32),
        in_specs=[anywhere] * 5,
        out_specs=vector,
        scratch_shapes=[
            pltpu.VMEM((1, nvir), jnp.int32),
            pltpu.SMEM((1, nvir), jnp.int32),
            pltpu.SMEM((1, IRREPS - 1), jnp.int32),
            pltpu.SMEM((cols, rows), jnp.int32),
            pltpu.VMEM((rows, pair_rows, amp_cols // rows), BF16),
            pltpu.VMEM((slab_rows, panel), BF16),
            pltpu.VMEM((rows - 1, pair_rows, kept), BF16),
            pltpu.VMEM((rows, pair_rows, kept), BF16),
            pltpu.VMEM((cols, kept, panel), BF16),
            pltpu.VMEM((rows, pair_rows, live), F32),
            pltpu.VMEM((rows, pair_rows, live), F32),
            dma((4 + slab_rows // nvir + rows,)),
            dma((rows,)),
            dma((rows,)),
            dma((cols, slab_rows // nvir)),
            dma((cols, slab_rows // nvir)),
            dma((rows,)),
            dma((rows,)),
        ],
        compiler_params=pltpu.CompilerParams(
            collective_id=0, has_side_effects=True, vmem_limit_bytes=62 * 1024 * 1024
        ),
    )(
        amplitudes, integrals, vir_irrep.reshape(1, nvir), occ_starts.reshape(1, -1), panel_owner.T,
    )


def solution(mesh):
    in_specs = (P(("row", "col"), None), P("row", "col"), P(), P(), P())
    out_specs = P(("row", "col"), None)
    return jax.shard_map(body, mesh=mesh, in_specs=in_specs, out_specs=out_specs, check_vma=False)
```
